128 devices in a mesh: row: 8 (over z, core), col: 8 (over x, y_lo), depth: 2 (over y_hi).
Axes of the slice: x: 4, y: 4 (y_hi: 2, y_lo: 2; y = y_hi * 2 + y_lo), z: 4, core: 2. Of those that a mesh axis runs over, the one named last changes fastest.
Arguments:
- hidden_state: bfloat16 [2048, 8192], P(('col', 'depth'), 'row'), may hold values from -110 to 110
- norm_gain: float32 [8192], P('row'), may hold values from 0.1 to 1.9
- gate_up_weight: bfloat16 [8192, 2, 28672], P('row', None, ('col', 'depth')), may hold values from -0.0625 to 0.0625
- down_weight: bfloat16 [28672, 8192], P(('col', 'depth'), 'row'), may hold values from -0.03125 to 0.03125
Outputs:
- block_output: bfloat16 [2048, 8192], P(('col', 'depth'), 'row')
The draws below stay inside these ranges and needn't reach their ends.
All inputs are finite; a program needn't handle non-finite values.
Results may differ from the reference program's by a relative error of at most 0.014.
Values may be sent and summed in bfloat16 or wider, within the bound.
A program may use at most 128 MiB of HBM per device.

```python
import jax
import jax.numpy as jnp
from jax import lax

D = 8192
FF = 28672
TOKENS = 2048
N_ROW = 8


def draw_hidden_state(key, part):
    key = jax.random.fold_in(key, 11)
    first, second, third = jax.random.split(key, 3)
    place = jnp.arange(D, dtype=jnp.float32) / D
    base = jnp.clip(jax.random.normal(first, (TOKENS, D), jnp.float32), -6.0, 6.0)
    rows = jnp.power(10.0, jax.random.uniform(second, (TOKENS, 1), jnp.float32, -0.5, 0.5))
    cols = jnp.power(10.0, jax.random.uniform(third, (1, D), jnp.float32, -0.5, 0.5)) * jnp.power(3.0, 0.5 * (place - 0.5))[None, :]
    return (base * rows * cols).astype(jnp.bfloat16)


def block_scale(key, extent, cuts, low, high):
    level = 1.0
    for dim, parts in cuts:
        heights = jax.random.uniform(jax.random.fold_in(jax.random.fold_in(key, 6), dim), (parts,), jnp.float32, low / len(cuts), high / len(cuts))
        level = level * jnp.repeat(jnp.exp(heights), extent[dim] // parts).reshape((-1,) + (1,) * (len(extent) - 1 - dim))
    return level


def gaussian(stream_key, extent, deviation, bound, shards=(), kind=jnp.bfloat16):
    entries = deviation * jax.random.normal(stream_key, extent, jnp.float32)
    if shards:
        entries = entries * block_scale(stream_key, extent, shards, -0.22, 0.18)
    return jnp.clip(entries, -bound, bound).astype(kind)


def setup_inputs(seed: int = 0) -> dict:
    key_list = jax.random.split(jax.random.key(seed), 5)
    hidden_state = draw_hidden_state(jax.random.fold_in(key_list[4], 71), 0)
    norm_gain = jnp.clip(1.0 + 0.18 * jax.random.normal(key_list[1], (D,), jnp.float32), 0.1, 1.9)
    gate_up_weight = gaussian(key_list[2], (D, 2, FF), D ** -0.5, 0.0625, ((0, 8), (2, 16)))
    down_weight = gaussian(key_list[3], (FF, D), FF ** -0.5, 0.03125, ((0, 16), (1, 8)))
    return {"hidden_state": hidden_state, "norm_gain": norm_gain, "gate_up_weight": gate_up_weight, "down_weight": down_weight}


def reference(hidden_state, norm_gain, gate_up_weight, down_weight):
    wide = hidden_state.astype(jnp.float32)
    squares = lax.optimization_barrier(jnp.sum(wide * wide, axis=1))
    scale = lax.rsqrt(squares / D + 1e-05)
    normed = (wide * scale[:, None] * norm_gain[None, :]).astype(jnp.bfloat16)
    width = D // N_ROW
    blocks_in = jnp.moveaxis(normed.reshape(TOKENS, N_ROW, width), 1, 0)
    blocks_w = gate_up_weight.reshape(N_ROW, width, 2 * FF)

    def add_block(total, pair):
        term = jnp.dot(pair[0], pair[1], preferred_element_type=jnp.float32).astype(jnp.bfloat16)
        term = lax.optimization_barrier(term)
        return (total + term.astype(jnp.float32), None)
    start = jnp.zeros((TOKENS, 2 * FF), jnp.float32)
    gate_up, unused = lax.scan(add_block, start, (blocks_in, blocks_w))
    gate_up = gate_up.reshape(TOKENS, 2, FF)
    hidden = (jax.nn.silu(gate_up[:, 0]) * gate_up[:, 1]).astype(jnp.bfloat16)
    branch = jnp.dot(hidden, down_weight, preferred_element_type=jnp.float32)
    return (wide + branch).astype(jnp.bfloat16)
```

```python
import functools

import jax
import jax.numpy as jnp
from jax import lax
from jax.experimental import pallas as pl
from jax.experimental.pallas import tpu as pltpu
from jax.sharding import PartitionSpec as P

D = 8192
TOK = 128
KB = 1024
FH = 896
STEPS = 16
ROWS = TOK // 4
LAST = STEPS - 1
MESH = pl.DeviceIdType.MESH
BF, F32 = jnp.bfloat16, jnp.float32


def kernel(
    h_ref, gain_ref, wt_ref, wd_ref, out_ref,
    a, w, wd, s, br, cs, hid, ds, dr, acc, sq,
    sq_send, sq_recv, a_send, a_recv, as_send, as_recv,
    w_local, w_send, w_recv, wd_sem,
    b_send, b_recv, c_send, c_recv, cs_send, hs_send, hs_recv, d_send, d_recv,
):
    col, depth, row = lax.axis_index("col"), lax.axis_index("depth"), lax.axis_index("row")
    x, y = col // 2, depth * 2 + col % 2
    z, c = row // 2, row % 2

    def at_xy(nx, ny):
        nx, ny = lax.rem(nx + 8, 4), lax.rem(ny + 8, 4)
        return {"col": nx * 2 + ny % 2, "depth": ny // 2}

    def at_z(d, other=0):
        core = c if not other else 1 - c
        return {"row": lax.rem(z + d + 4, 4) * 2 + core}

    sibling = at_z(0, 1)

    def prim(d):
        return at_xy(x + d * (1 - c), y + d * c)

    def sec(d):
        return at_xy(x + d * c, y + d * (1 - c))

    def slot(p, q):
        dx = p * (1 - c) + q * c
        dy = q * (1 - c) + p * c
        return lax.rem(dx + 4 * dy + 15, 16)

    def rdma(src, dst, ssem, rsem, dev):
        return pltpu.make_async_remote_copy(
            src_ref=src, dst_ref=dst, send_sem=ssem, recv_sem=rsem, device_id=dev, device_id_type=MESH
        )

    def wait_recv(ref, sem, dev=sibling):
        rdma(ref, ref, a_send, sem, dev).wait_recv()

    def wait_send(ref, sem, dev=sibling):
        rdma(ref, ref, sem, sem, dev).wait_send()

    barrier = pltpu.get_barrier_semaphore()
    peers = [at_xy(x + o % 4, y + o // 4) for o in range(1, 16)]
    rows = [{"row": lax.rem(row + d, 8)} for d in range(1, 8)]

    own_w = [
        pltpu.make_async_copy(
            wt_ref.at[g, :, pl.ds(pl.multiple_of(c * FH, 128), FH)],
            w.at[c, :, g * FH:(g + 1) * FH],
            w_local.at[g],
        )
        for g in range(2)
    ]
    for copy in own_w:
        copy.start()
    own_wd = pltpu.make_async_copy(wd_ref, wd, wd_sem)
    own_wd.start()

    for dev in peers + rows:
        pl.semaphore_signal(barrier, inc=1, device_id=dev, device_id_type=MESH)

    part = jnp.zeros((TOK, 128), F32)
    for k in range(KB // 128):
        v = h_ref[:, k * 128:(k + 1) * 128].astype(F32)
        acc[:, k * 128:(k + 1) * 128] = v
        part = part + v * v
    sums = jnp.sum(part.T, axis=0, keepdims=True)
    sq[row] = jnp.broadcast_to(sums, (8, 128))

    pl.semaphore_wait(barrier, len(peers) + len(rows))

    for dev in rows:
        rdma(sq.at[row], sq.at[row], sq_send, sq_recv.at[row], dev).start()
    for g in range(2):
        rdma(
            wt_ref.at[g, :, pl.ds(pl.multiple_of((1 - c) * FH, 128), FH)],
            w.at[c, :, g * FH:(g + 1) * FH],
            w_send.at[g],
            w_recv.at[g],
            sibling,
        ).start()
    for d in range(1, 8):
        r = lax.rem(row + d, 8)
        wait_recv(sq.at[r], sq_recv.at[r])
    total = sq[0]
    for r in range(1, 8):
        total = total + sq[r]
    scale = lax.rsqrt(total[0:1] / D + 1e-05)
    scale = jnp.broadcast_to(scale, (128, 128)).T
    for k in range(KB // 128):
        cols = slice(k * 128, (k + 1) * 128)
        a[LAST, c, :, cols] = (acc[:, cols] * scale * gain_ref[0:1, cols]).astype(BF)

    half = TOK // 2

    def whole(src, dst, dev):
        rdma(a.at[src, c], a.at[dst, c], a_send, a_recv.at[dst, 0], dev).start()

    def piece(src, dst, dev, n):
        r = slice(n * half, (n + 1) * half)
        rdma(a.at[src, c, r], a.at[dst, c, r], a_send, a_recv.at[dst, n], dev).start()

    def share(src):
        rdma(a.at[src, c], a.at[src, c], as_send, as_recv.at[src], sibling).start()

    def got(at):
        wait_recv(a.at[at, c], a_recv.at[at, 0])

    def got_halves(at):
        for n in range(2):
            wait_recv(a.at[at, c, n * half:(n + 1) * half], a_recv.at[at, n])

    def spread(p):
        at = slot(p, 0)
        whole(at, slot(p, 3), sec(1))
        whole(at, slot(p, 1), sec(-1))

    def turn(p, q):
        at = slot(p, q)
        got(at)
        share(at)
        if q == 1:
            piece(at, slot(p, 2), sec(-1), 0)
        else:
            piece(at, slot(p, 2), sec(1), 1)

    whole(LAST, slot(3, 0), prim(1))
    whole(LAST, slot(1, 0), prim(-1))
    spread(0)
    share(LAST)

    def events0():
        for p in (1, 3):
            at = slot(p, 0)
            got(at)
            share(at)
            if p == 1:
                piece(at, slot(2, 0), prim(-1), 0)
            else:
                piece(at, slot(2, 0), prim(1), 1)
        for q in (1, 3):
            turn(0, q)
        for p in (1, 3):
            spread(p)

    def events1():
        got_halves(slot(2, 0))
        share(slot(2, 0))
        spread(2)
        got_halves(slot(0, 2))
        share(slot(0, 2))

    def events2():
        for p in (1, 3):
            for q in (1, 3):
                turn(p, q)

    def events3():
        for q in (1, 3):
            turn(2, q)
        for p in (1, 3):
            got_halves(slot(p, 2))
            share(slot(p, 2))

    def events4():
        got_halves(slot(2, 2))
        share(slot(2, 2))

    events0()
    for copy in own_w:
        copy.wait()
    for g in range(2):
        wait_recv(w.at[1 - c, :, g * FH:(g + 1) * FH], w_recv.at[g])

    def rows_of(d):
        return pl.ds(pl.multiple_of(lax.rem(z + d + 4, 4) * ROWS, ROWS), ROWS)

    gate, up = slice(0, FH), slice(FH, 2 * FH)
    mine = pl.ds(pl.multiple_of(c * FH, 128), FH)

    def first_matmul(i):
        wait_recv(a.at[i, 1 - c], as_recv.at[i])

        @pl.loop(0, 2 * FH // 256)
        def _(n):
            cols = pl.ds(pl.multiple_of(n * 256, 256), 256)
            p = jnp.dot(a[i, 0], w[0, :, cols], preferred_element_type=F32)
            p += jnp.dot(a[i, 1], w[1, :, cols], preferred_element_type=F32)
            s[i, :, cols] = p.astype(BF)

        rdma(s.at[i, rows_of(2), gate], br.at[i, 0], b_send, b_recv.at[i, 0], at_z(1)).start()
        rdma(s.at[i, rows_of(2), up], br.at[i, 1], b_send, b_recv.at[i, 1], at_z(-1)).start()
        rdma(s.at[i, rows_of(1), up], br.at[i, 2], b_send, b_recv.at[i, 2], at_z(1)).start()
        rdma(s.at[i, rows_of(-1), gate], br.at[i, 3], b_send, b_recv.at[i, 3], at_z(-1)).start()

    def combine(i):
        for n, d, cols in ((0, 1, gate), (1, -1, up)):
            wait_recv(br.at[i, n], b_recv.at[i, n])
            cs[i, n] = (s[i, rows_of(d), cols].astype(F32) + br[i, n].astype(F32)).astype(BF)
            rdma(cs.at[i, n], br.at[i, 4 + n], cs_send, b_recv.at[i, 4 + n], at_z(d)).start()

    def finish(i):
        for n in (2, 3, 4, 5):
            wait_recv(br.at[i, n], b_recv.at[i, n])
        g = s[i, rows_of(0), gate].astype(F32) + br[i, 4].astype(F32) + br[i, 3].astype(F32)
        u = s[i, rows_of(0), up].astype(F32) + br[i, 5].astype(F32) + br[i, 2].astype(F32)
        hid[i, rows_of(0), mine] = (g / (1.0 + jnp.exp(-g)) * u).astype(BF)
        block = hid.at[i, rows_of(0), mine]
        rdma(block, block, c_send, c_recv.at[i, 0], at_z(1)).start()
        rdma(block, block, c_send, c_recv.at[i, 1], at_z(-1)).start()

    def half_rows(d, n):
        return pl.ds(pl.multiple_of(lax.rem(z + d + 4, 4) * ROWS + n * 16, 16), 16)

    def forward(i):
        for n, d in ((0, -1), (1, 1)):
            wait_recv(hid.at[i, rows_of(d), mine], c_recv.at[i, n])
            block = hid.at[i, half_rows(d, n), mine]
            rdma(block, block, c_send, c_recv.at[i, 2 + n], at_z(-d)).start()

    def pair(i):
        for n in (0, 1):
            wait_recv(hid.at[i, half_rows(2, n), mine], c_recv.at[i, 2 + n])
        block = hid.at[i, :, mine]
        rdma(block, block, hs_send, hs_recv.at[i], sibling).start()

    def second_matmul(i):
        other = pl.ds(pl.multiple_of((1 - c) * FH, 128), FH)
        wait_recv(hid.at[i, :, other], hs_recv.at[i])

        @pl.loop(0, KB // 256)
        def _(n):
            cols = pl.ds(pl.multiple_of(n * 256, 256), 256)
            t = jnp.dot(hid[i], wd[:, cols], preferred_element_type=F32)
            ds[i, :, cols] = t.astype(BF)

        @pl.when(i < LAST)
        def _():
            o = i + 1
            dev = at_xy(x + o % 4, y + o // 4)
            rdma(ds.at[i], dr.at[i], d_send, d_recv.at[i], dev).start()

    def gather_sum(i):
        wait_recv(dr.at[i], d_recv.at[i])
        acc[...] += dr[i].astype(F32)

    def at(i, low, high, body):
        @pl.when(jnp.logical_and(i >= low, i < high))
        def _():
            body(i - low)

    def step(t, carry):
        pl.when(t == 1)(events1)
        pl.when(t == 2)(events2)
        pl.when(t == 3)(events3)
        pl.when(t == 6)(events4)
        at(t, 0, STEPS, first_matmul)
        at(t, 1, STEPS + 1, combine)
        at(t, 2, STEPS + 2, finish)
        at(t, 3, STEPS + 3, forward)
        at(t, 4, STEPS + 4, pair)
        pl.when(t == 5)(own_wd.wait)
        at(t, 5, STEPS + 5, second_matmul)
        at(t, 7, LAST + 7, gather_sum)
        return carry

    lax.fori_loop(0, LAST + 7, step, 0)
    out_ref[...] = (acc[...] + ds[LAST].astype(F32)).astype(BF)

    for _ in rows:
        pass
    wait_send(sq.at[0:7], sq_send)
    for g in range(2):
        wait_send(w.at[c, :, g * FH:(g + 1) * FH], w_send.at[g])
    wait_send(a.at[0:15, c], a_send)
    wait_send(a.at[:, c], as_send)
    wait_send(s.at[:, :, gate], b_send)
    wait_send(cs, cs_send)
    wait_send(hid.at[:, 0:3 * ROWS, gate], c_send)
    wait_send(hid.at[:, :, gate], hs_send)
    wait_send(ds.at[0:LAST], d_send)


def local(hidden_state, norm_gain, gate_up_weight, down_weight):
    wt = jnp.transpose(gate_up_weight, (1, 0, 2))
    dma = pltpu.SemaphoreType.DMA
    any_, vmem = pl.BlockSpec(memory_space=pl.ANY), pl.BlockSpec(memory_space=pltpu.VMEM)
    return pl.pallas_call(
        kernel,
        out_shape=jax.ShapeDtypeStruct((TOK, KB), BF),
        in_specs=[vmem, vmem, any_, any_],
        out_specs=vmem,
        scratch_shapes=[
            pltpu.VMEM((STEPS, 2, TOK, KB), BF),
            pltpu.VMEM((2, KB, 2 * FH), BF),
            pltpu.VMEM((2 * FH, KB), BF),
            pltpu.VMEM((STEPS, TOK, 2 * FH), BF),
            pltpu.VMEM((STEPS, 6, ROWS, FH), BF),
            pltpu.VMEM((STEPS, 2, ROWS, FH), BF),
            pltpu.VMEM((STEPS, TOK, 2 * FH), BF),
            pltpu.VMEM((STEPS, TOK, KB), BF),
            pltpu.VMEM((LAST, TOK, KB), BF),
            pltpu.VMEM((TOK, KB), F32),
            pltpu.VMEM((8, 8, 128), F32),
            dma, dma((8,)), dma, dma((STEPS, 2)), dma, dma((STEPS,)),
            dma((2,)), dma((2,)), dma((2,)), dma,
            dma, dma((STEPS, 6)), dma, dma((STEPS, 4)), dma, dma, dma((STEPS,)), dma, dma((STEPS,)),
        ],
        compiler_params=pltpu.CompilerParams(
            collective_id=0, has_side_effects=True, vmem_limit_bytes=60 * 1024 * 1024
        ),
    )(hidden_state, norm_gain.reshape(1, KB), wt, down_weight)


def solution(mesh):
    return jax.shard_map(
        local,
        mesh=mesh,
        in_specs=(
            P(("col", "depth"), "row"),
            P("row"),
            P("row", None, ("col", "depth")),
            P(("col", "depth"), "row"),
        ),
        out_specs=P(("col", "depth"), "row"),
        check_vma=False,
    )
```

```python
import functools

import jax
import jax.numpy as jnp
from jax import lax
from jax.experimental import pallas as pl
from jax.experimental.pallas import tpu as pltpu
from jax.sharding import PartitionSpec as P

D = 8192
TOK = 128
KB = 1024
FH = 896
STEPS = 16
COMBINE, FINISH, FORWARD, PAIR, LAG = 2, 3, 4, 5, 6
ROWS = TOK // 4
OWN = 0
MESH = pl.DeviceIdType.MESH
BF, F32 = jnp.bfloat16, jnp.float32


def kernel(
    h_ref, gain_ref, wg_ref, wd_ref, out_ref,
    a, raw, w, wd, s, br, cs, hid, ds, df, dn, ys, xf, xn, acc, sq, sc,
    sq_send, sq_recv, sc_send, sc_recv, a_send, a_recv, as_send, as_recv,
    w_local, w_send, w_recv, wd_sem,
    b_send, b_recv, c_send, c_recv, cs_send, hs_send, hs_recv, d_send, y_recv, x_recv,
):
    col, depth, row = lax.axis_index("col"), lax.axis_index("depth"), lax.axis_index("row")
    x, y = col // 2, depth * 2 + col % 2
    z, c = row // 2, row % 2

    def at_xy(nx, ny):
        nx, ny = lax.rem(nx + 8, 4), lax.rem(ny + 8, 4)
        return {"col": nx * 2 + ny % 2, "depth": ny // 2}

    def at_z(d, other=0):
        core = c if not other else 1 - c
        return {"row": lax.rem(z + d + 4, 4) * 2 + core}

    sibling = at_z(0, 1)

    def rdma(src, dst, ssem, rsem, dev):
        return pltpu.make_async_remote_copy(
            src_ref=src, dst_ref=dst, send_sem=ssem, recv_sem=rsem, device_id=dev, device_id_type=MESH
        )

    def wait_recv(ref, sem, dev=sibling):
        rdma(ref, ref, a_send, sem, dev).wait_recv()

    def wait_send(ref, sem, dev=sibling):
        rdma(ref, ref, sem, sem, dev).wait_send()

    def wide(v):
        return v.astype(F32)

    barrier = pltpu.get_barrier_semaphore()
    plane = range(1, 16)
    peers = [at_xy(x + o // 4, y + o % 4) for o in plane]
    rows = [{"row": lax.rem(row + d, 8)} for d in range(1, 8)]

    def columns(core):
        return pl.ds(pl.multiple_of(core * FH, 128), FH)

    own_w = pltpu.make_async_copy(wg_ref.at[:, :, columns(c)], raw.at[c], w_local)
    own_w.start()
    own_wd = pltpu.make_async_copy(wd_ref, wd, wd_sem)
    own_wd.start()

    for dev in peers + rows:
        pl.semaphore_signal(barrier, inc=1, device_id=dev, device_id_type=MESH)

    lanes = jnp.zeros((TOK, 128), F32)
    for k in range(KB // 128):
        cols = slice(k * 128, (k + 1) * 128)
        v = h_ref[:, cols].astype(F32)
        a[OWN, c, :, cols] = (v * gain_ref[0:1, cols]).astype(BF)
        acc[:, cols] = v
        lanes = lanes + v * v
    sums = jnp.sum(lanes.T, axis=0, keepdims=True)
    sq[row] = jnp.broadcast_to(sums, (8, 128))

    pl.semaphore_wait(barrier, len(peers) + len(rows))

    half = TOK // 2

    def slot(dx, dy):
        return dx % 4 * 4 + dy % 4

    def place(dx, dy, n):
        dx = dx % 4
        return (slot(1 + 2 * n, dy), dx // 2) if dx % 2 else (slot(dx, dy), n)

    def part(at, n):
        return a.at[at, c, n * half:(n + 1) * half]

    def hop(dx, dy, n, ox, oy):
        dst = place(dx - ox, dy - oy, n)
        dev = at_xy(x + ox, y + oy)
        rdma(part(*place(dx, dy, n)), part(*dst), a_send, a_recv.at[dst[0], dst[1]], dev).start()

    def share(at):
        rdma(a.at[at, c], a.at[at, c], as_send, as_recv.at[at], sibling).start()

    def got(at, n):
        wait_recv(part(at, n), a_recv.at[at, n])

    def have(dx, dy):
        at = slot(dx, dy)
        got(at, 0)
        got(at, 1)
        share(at)

    def spread_y(*halves):
        for oy in (1, -1):
            for dx, n in halves:
                hop(dx, 0, n, 0, oy)

    def spread_x(dy, n):
        hop(0, dy, n, -1, 0)
        hop(0, dy, n, 1, 0)

    def first_x(k):
        if k == 0:
            spread_x(0, 0)
            spread_x(0, 1)
        elif k == 1:
            have(1, 0)
            spread_y((1, 0), (3, 0))
        elif k == 2:
            share(OWN)
            have(1, 1)
            hop(1, 1, 0, 0, -1)
            hop(3, 1, 0, 0, -1)
            have(3, 0)
            spread_y((1, 1), (3, 1))
            have(1, 3)
            hop(1, 0, 0, -1, 0)
            hop(3, 0, 1, 1, 0)
        elif k == 3:
            have(1, 2)
            have(3, 3)
            hop(1, 3, 1, 0, 1)
            hop(3, 3, 1, 0, 1)
            have(3, 1)
        elif k == 4:
            have(2, 0)
            spread_y((2, 0), (2, 1))
            have(3, 2)
        elif k == 5:
            have(2, 1)
            hop(2, 1, 0, 0, -1)
            have(2, 3)
            hop(2, 3, 1, 0, 1)
            spread_y((0, 0), (0, 1))
        elif k == 6:
            have(0, 1)
            hop(0, 1, 0, 0, -1)
            have(0, 3)
            hop(0, 3, 1, 0, 1)
        elif k == 7:
            have(2, 2)
        elif k == 8:
            have(0, 2)

    def first_y(k):
        if k == 0:
            spread_x(0, 0)
            spread_y((0, 0))
            spread_y((0, 1))
            spread_x(0, 1)
        elif k == 1:
            have(1, 0)
            got(slot(0, 1), 0)
            spread_x(1, 0)
            hop(0, 1, 0, 0, -1)
            got(slot(0, 3), 0)
            spread_x(3, 0)
        elif k == 2:
            share(OWN)
            got(slot(0, 2), 0)
            spread_x(2, 0)
            for dy in (1, 3):
                got(slot(0, dy), 1)
                share(slot(0, dy))
                spread_x(dy, 1)
            hop(0, 3, 1, 0, 1)
            have(1, 1)
            have(1, 3)
        elif k == 3:
            got(slot(0, 2), 1)
            share(slot(0, 2))
            spread_x(2, 1)
            have(1, 2)
            have(3, 0)
            for dy in (0, 1, 3, 2):
                hop(1, dy, 0, -1, 0)
        elif k == 4:
            for dy in (1, 3, 2):
                have(3, dy)
            for dy in (0, 1, 3, 2):
                hop(3, dy, 1, 1, 0)
        elif k == 7:
            for dy in (2, 1, 3, 0):
                have(2, dy)

    def gather(k):
        pl.when(c == 0)(functools.partial(first_x, k))
        pl.when(c == 1)(functools.partial(first_y, k))

    gather(0)
    for dev in rows:
        rdma(sq.at[row], sq.at[row], sq_send, sq_recv.at[row], dev).start()
    rdma(wg_ref.at[:, :, columns(1 - c)], raw.at[c], w_send, w_recv, sibling).start()

    def deal(core):
        @pl.loop(0, KB // 64)
        def _(n):
            ks = pl.ds(pl.multiple_of(n * 64, 64), 64)
            both = jnp.swapaxes(raw[core, ks], 0, 1)
            w[core, ks, 0:FH] = both[0]
            w[core, ks, FH:2 * FH] = both[1]

    own_w.wait()
    deal(c)
    def digit(n):
        return (1 + 3 * (n % 2)) * (1 + 15 * (n // 2))

    def offsets(i):
        g, j = i // 4, i % 4
        far_first = g // 2
        order = 180 - 126 * far_first
        dx = 45 // digit(g) % 4
        dy = order // digit(j) % 4
        return dx, dy

    def rows_of(d):
        return pl.ds(pl.multiple_of(lax.rem(z + d + 4, 4) * ROWS, ROWS), ROWS)

    def scales():
        for d in range(1, 8):
            r = lax.rem(row + d, 8)
            wait_recv(sq.at[r], sq_recv.at[r])
        total = sq[0]
        for r in range(1, 8):
            total = total + sq[r]
        scale = jnp.broadcast_to(lax.rsqrt(total[0:1] / D + 1e-05), (128, 128)).T
        for q in range(4):
            sc[OWN, q] = scale[q * ROWS:(q + 1) * ROWS]

        def give(dx, dy, q, n):
            dst = lax.rem(dx + 4, 4) * 4 + dy
            dev = at_xy(x - dx, y - dy)
            rdma(sc.at[OWN, q], sc.at[dst, q], sc_send, sc_recv.at[dst, n], dev).start()

        for dy in range(4):
            for n in range(2):
                give(1 + 2 * (z // 2), dy, 2 * n + z % 2, n)
        for dx, dy in ((2, 0), (2, 1), (2, 2), (2, 3), (0, 1), (0, 2), (0, 3)):
            give(dx, dy, z, 0)

    gather(1)
    wait_recv(raw.at[1 - c], w_recv)
    deal(1 - c)

    gate, up = slice(0, FH), slice(FH, 2 * FH)
    mine = columns(c)

    def first_matmul(i):
        dx, dy = offsets(i)
        at = dx * 4 + dy
        wait_recv(a.at[at, 1 - c], as_recv.at[at])

        @pl.loop(0, 2 * FH // 256)
        def _(n):
            cols = pl.ds(pl.multiple_of(n * 256, 256), 256)
            p = jnp.dot(a[at, 0], w[0, :, cols], preferred_element_type=F32)
            p += jnp.dot(a[at, 1], w[1, :, cols], preferred_element_type=F32)
            s[i, :, cols] = p.astype(BF)

        rdma(s.at[i, rows_of(2), gate], br.at[i, 0], b_send, b_recv.at[i, 0], at_z(1)).start()
        rdma(s.at[i, rows_of(2), up], br.at[i, 1], b_send, b_recv.at[i, 1], at_z(-1)).start()
        rdma(s.at[i, rows_of(1), up], br.at[i, 2], b_send, b_recv.at[i, 2], at_z(1)).start()
        rdma(s.at[i, rows_of(-1), gate], br.at[i, 3], b_send, b_recv.at[i, 3], at_z(-1)).start()

    def combine(i):
        for n, d, cols in ((0, 1, gate), (1, -1, up)):
            wait_recv(br.at[i, n], b_recv.at[i, n])
            cs[i, n] = (s[i, rows_of(d), cols].astype(F32) + br[i, n].astype(F32)).astype(BF)
            rdma(cs.at[i, n], br.at[i, 4 + n], cs_send, b_recv.at[i, 4 + n], at_z(d)).start()

    def finish(i):
        for n in (2, 3, 4, 5):
            wait_recv(br.at[i, n], b_recv.at[i, n])
        dx, dy = offsets(i)
        mixed, n = 1 - i // 8, i // 4
        at = (mixed * (1 + 2 * (z // 2)) + (1 - mixed) * dx) * 4 + dy
        q = mixed * (2 * n + z % 2) + (1 - mixed) * z

        @pl.when(at != OWN)
        def _():
            wait_recv(sc.at[at, q], sc_recv.at[at, mixed * n])

        scale = sc[at, q]
        for k in range(FH // 128):
            cols = slice(k * 128, (k + 1) * 128)
            ups = slice(FH + k * 128, FH + (k + 1) * 128)
            g = (wide(s[i, rows_of(0), cols]) + wide(br[i, 4, :, cols]) + wide(br[i, 3, :, cols])) * scale
            u = (wide(s[i, rows_of(0), ups]) + wide(br[i, 5, :, cols]) + wide(br[i, 2, :, cols])) * scale
            to = pl.ds(pl.multiple_of(c * FH + k * 128, 128), 128)
            hid[i, rows_of(0), to] = (g / (1.0 + jnp.exp(-g)) * u).astype(BF)
        block = hid.at[i, rows_of(0), mine]
        rdma(block, block, c_send, c_recv.at[i, 0], at_z(1)).start()
        rdma(block, block, c_send, c_recv.at[i, 1], at_z(-1)).start()

    def half_rows(d, n):
        return pl.ds(pl.multiple_of(lax.rem(z + d + 4, 4) * ROWS + n * 16, 16), 16)

    def forward(i):
        for n, d in ((0, -1), (1, 1)):
            wait_recv(hid.at[i, rows_of(d), mine], c_recv.at[i, n])
            block = hid.at[i, half_rows(d, n), mine]
            rdma(block, block, c_send, c_recv.at[i, 2 + n], at_z(-d)).start()

    def pair(i):
        for n in (0, 1):
            wait_recv(hid.at[i, half_rows(2, n), mine], c_recv.at[i, 2 + n])
        block = hid.at[i, :, mine]
        rdma(block, block, hs_send, hs_recv.at[i], sibling).start()

    def second_matmul(i):
        wait_recv(hid.at[i, :, columns(1 - c)], hs_recv.at[i])

        @pl.loop(0, KB // 256)
        def _(n):
            cols = pl.ds(pl.multiple_of(n * 256, 256), 256)
            t = jnp.dot(hid[i], wd[:, cols], preferred_element_type=F32)
            ds[i, :, cols] = t.astype(BF)

    def ring(d):
        return at_xy(x, y + d)

    def line(d):
        return at_xy(x + d, y)

    top, low = slice(0, half), slice(half, TOK)

    def y_far(g, i):
        rdma(ds.at[i, top], df.at[g, 0], d_send, y_recv.at[g, 0], ring(1)).start()
        rdma(ds.at[i, low], df.at[g, 1], d_send, y_recv.at[g, 1], ring(-1)).start()

    def y_near(g, i, n):
        rows = (top, low)[n]
        wait_recv(df.at[g, n], y_recv.at[g, n])
        ds[i, rows] = (wide(ds[i, rows]) + wide(df[g, n])).astype(BF)
        rdma(ds.at[i], dn.at[g, n], d_send, y_recv.at[g, 2 + n], ring(1 - 2 * n)).start()

    def y_sum(g, i):
        for n in range(2):
            wait_recv(dn.at[g, n], y_recv.at[g, 2 + n])
        ys[g] = (wide(ds[i]) + wide(dn[g, 0]) + wide(dn[g, 1])).astype(BF)

    def x_far():
        rdma(ys.at[2, top], xf.at[0], d_send, x_recv.at[0], line(1)).start()
        rdma(ys.at[2, low], xf.at[1], d_send, x_recv.at[1], line(-1)).start()

    def x_near(n):
        rows = (top, low)[n]
        wait_recv(xf.at[n], x_recv.at[n])
        ys[n, rows] = (wide(ys[n, rows]) + wide(xf[n])).astype(BF)
        for m in range(2):
            to = xn.at[n, (top, low)[m]]
            rdma(ys.at[m, rows], to, d_send, x_recv.at[2 + 2 * n + m], line(1 - 2 * n)).start()

    def branch_sums(t):
        def when(n, *bodies):
            @pl.when(t == LAG + n)
            def _():
                for body in bodies:
                    body()

        call = functools.partial
        for g in (0, 1):
            i = 4 * g
            when(i + 3, call(y_far, g, i + 3))
            when(i + 4, call(y_near, g, i + 1, 0), call(y_near, g, i + 2, 1))
            when(i + 6, call(y_sum, g, i))
        for g in (2, 3):
            i = 4 * g
            when(i, call(y_far, g, i))
            when(i + 1, call(y_near, g, i + 1, 0))
            when(i + 2, call(y_near, g, i + 2, 1))
        when(11, call(y_sum, 2, 11), x_far)
        when(13, call(x_near, 0), call(x_near, 1))

    def at(i, low, high, body):
        @pl.when(jnp.logical_and(i >= low, i < high))
        def _():
            body(i - low)

    def step(t, carry):
        pl.when(t == 1)(scales)
        at(t, COMBINE, STEPS + COMBINE, combine)
        at(t, FINISH, STEPS + FINISH, finish)
        at(t, FORWARD, STEPS + FORWARD, forward)
        at(t, PAIR, STEPS + PAIR, pair)
        for k in range(2, 9):
            pl.when(t == k - 1)(functools.partial(gather, k))
        at(t, 0, STEPS, first_matmul)
        pl.when(t == LAG)(own_wd.wait)
        at(t, LAG, STEPS + LAG, second_matmul)
        branch_sums(t)
        return carry

    lax.fori_loop(0, STEPS + LAG, step, 0)
    total = acc[...] + wide(ds[STEPS - 1])
    for n in range(2):
        for m in range(2):
            wait_recv(xn.at[n, (top, low)[m]], x_recv.at[2 + 2 * n + m])
        total += wide(xn[n])
    for n in range(2):
        wait_recv(dn.at[3, n], y_recv.at[3, 2 + n])
        total += wide(dn[3, n])
    out_ref[...] = total.astype(BF)

    wait_send(sq.at[0:7], sq_send)
    wait_send(raw.at[c], w_send)
    wait_send(sc.at[1:16, 0], sc_send)
    wait_send(a.at[0:15, c], a_send)
    wait_send(a.at[:, c], as_send)
    wait_send(s.at[:, :, gate], b_send)
    wait_send(cs, cs_send)
    wait_send(hid.at[:, 0:3 * ROWS, gate], c_send)
    wait_send(hid.at[:, :, gate], hs_send)
    wait_send(ds.at[0:15], d_send)


def local(hidden_state, norm_gain, gate_up_weight, down_weight):
    dma = pltpu.SemaphoreType.DMA
    any_, vmem = pl.BlockSpec(memory_space=pl.ANY), pl.BlockSpec(memory_space=pltpu.VMEM)
    return pl.pallas_call(
        kernel,
        out_shape=jax.ShapeDtypeStruct((TOK, KB), BF),
        in_specs=[vmem, vmem, any_, any_],
        out_specs=vmem,
        scratch_shapes=[
            pltpu.VMEM((STEPS, 2, TOK, KB), BF),
            pltpu.VMEM((2, KB, 2, FH), BF),
            pltpu.VMEM((2, KB, 2 * FH), BF),
            pltpu.VMEM((2 * FH, KB), BF),
            pltpu.VMEM((STEPS, TOK, 2 * FH), BF),
            pltpu.VMEM((STEPS, 6, ROWS, FH), BF),
            pltpu.VMEM((STEPS, 2, ROWS, FH), BF),
            pltpu.VMEM((STEPS, TOK, 2 * FH), BF),
            pltpu.VMEM((STEPS, TOK, KB), BF),
            pltpu.VMEM((4, 2, TOK // 2, KB), BF),
            pltpu.VMEM((4, 2, TOK, KB), BF),
            pltpu.VMEM((3, TOK, KB), BF),
            pltpu.VMEM((2, TOK // 2, KB), BF),
            pltpu.VMEM((2, TOK, KB), BF),
            pltpu.VMEM((TOK, KB), F32),
            pltpu.VMEM((8, 8, 128), F32),
            pltpu.VMEM((STEPS, 4, ROWS, 128), F32),
            dma, dma((8,)), dma, dma((STEPS, 2)), dma, dma((STEPS, 2)), dma, dma((STEPS,)),
            dma, dma, dma, dma,
            dma, dma((STEPS, 6)), dma, dma((STEPS, 4)), dma, dma, dma((STEPS,)), dma, dma((4, 4)), dma((6,)),
        ],
        compiler_params=pltpu.CompilerParams(
            collective_id=0, has_side_effects=True, vmem_limit_bytes=60 * 1024 * 1024
        ),
    )(hidden_state, norm_gain.reshape(1, KB), gate_up_weight, down_weight)


def solution(mesh):
    return jax.shard_map(
        local,
        mesh=mesh,
        in_specs=(
            P(("col", "depth"), "row"),
            P("row"),
            P("row", None, ("col", "depth")),
            P(("col", "depth"), "row"),
        ),
        out_specs=P(("col", "depth"), "row"),
        check_vma=False,
    )
```

```python
import functools

import jax
import jax.numpy as jnp
from jax import lax
from jax.experimental import pallas as pl
from jax.experimental.pallas import tpu as pltpu
from jax.sharding import PartitionSpec as P

D = 8192
TOK = 128
KB = 1024
FH = 896
STEPS = 16
COMBINE, FINISH, FORWARD, PAIR, LAG = 2, 3, 4, 5, 6
ROWS = TOK // 4
OWN = 0
MESH = pl.DeviceIdType.MESH
BF, F32 = jnp.bfloat16, jnp.float32


def kernel(
    h_ref, gain_ref, wg_ref, wd_ref, out_ref,
    a, raw, w, wd, s, br, cs, hid, ds, df, dn, ys, xf, xn, acc, sq, sc,
    sq_send, sq_recv, sc_send, sc_recv, a_send, a_recv, as_send, as_recv,
    w_local, w_send, w_recv, wd_sem,
    b_send, b_recv, c_send, c_recv, cs_send, hs_send, hs_recv, d_send, y_recv, x_recv,
):
    col, depth, row = lax.axis_index("col"), lax.axis_index("depth"), lax.axis_index("row")
    x, y = col // 2, depth * 2 + col % 2
    z, c = row // 2, row % 2

    def at_xy(nx, ny):
        nx, ny = lax.rem(nx + 8, 4), lax.rem(ny + 8, 4)
        return {"col": nx * 2 + ny % 2, "depth": ny // 2}

    def at_z(d, other=0):
        core = c if not other else 1 - c
        return {"row": lax.rem(z + d + 4, 4) * 2 + core}

    sibling = at_z(0, 1)

    def rdma(src, dst, ssem, rsem, dev):
        return pltpu.make_async_remote_copy(
            src_ref=src, dst_ref=dst, send_sem=ssem, recv_sem=rsem, device_id=dev, device_id_type=MESH
        )

    def wait_recv(ref, sem, dev=sibling):
        rdma(ref, ref, a_send, sem, dev).wait_recv()

    def wait_send(ref, sem, dev=sibling):
        rdma(ref, ref, sem, sem, dev).wait_send()

    def wide(v):
        return v.astype(F32)

    barrier = pltpu.get_barrier_semaphore()
    plane = range(1, 16)
    peers = [at_xy(x + o // 4, y + o % 4) for o in plane]
    rows = [{"row": lax.rem(row + d, 8)} for d in range(1, 8)]

    def columns(core):
        return pl.ds(pl.multiple_of(core * FH, 128), FH)

    own_w = pltpu.make_async_copy(wg_ref.at[:, :, columns(c)], raw.at[c], w_local)
    own_w.start()
    own_wd = pltpu.make_async_copy(wd_ref, wd, wd_sem)
    own_wd.start()

    for dev in peers + rows:
        pl.semaphore_signal(barrier, inc=1, device_id=dev, device_id_type=MESH)

    lanes = jnp.zeros((TOK, 128), F32)
    for k in range(KB // 128):
        cols = slice(k * 128, (k + 1) * 128)
        v = h_ref[:, cols].astype(F32)
        a[OWN, c, :, cols] = (v * gain_ref[0:1, cols]).astype(BF)
        acc[:, cols] = v
        lanes = lanes + v * v
    sums = jnp.sum(lanes.T, axis=0, keepdims=True)
    sq[row] = jnp.broadcast_to(sums, (8, 128))

    pl.semaphore_wait(barrier, len(peers) + len(rows))

    half = TOK // 2

    def slot(dx, dy):
        return dx % 4 * 4 + dy % 4

    def place(dx, dy, n):
        dx = dx % 4
        return (slot(1 + 2 * n, dy), dx // 2) if dx % 2 else (slot(dx, dy), n)

    def part(at, n):
        return a.at[at, c, n * half:(n + 1) * half]

    def hop(dx, dy, n, ox, oy):
        dst = place(dx - ox, dy - oy, n)
        dev = at_xy(x + ox, y + oy)
        rdma(part(*place(dx, dy, n)), part(*dst), a_send, a_recv.at[dst[0], dst[1]], dev).start()

    def share(at):
        rdma(a.at[at, c], a.at[at, c], as_send, as_recv.at[at], sibling).start()

    def got(at, n):
        wait_recv(part(at, n), a_recv.at[at, n])

    def have(dx, dy):
        at = slot(dx, dy)
        got(at, 0)
        got(at, 1)
        share(at)

    def spread_y(*halves):
        for oy in (1, -1):
            for dx, n in halves:
                hop(dx, 0, n, 0, oy)

    def spread_x(dy, n):
        hop(0, dy, n, -1, 0)
        hop(0, dy, n, 1, 0)

    def first_x(k):
        if k == 0:
            spread_x(0, 0)
            spread_x(0, 1)
        elif k == 1:
            have(1, 0)
            spread_y((1, 0), (3, 0))
        elif k == 2:
            share(OWN)
            have(1, 1)
            hop(1, 1, 0, 0, -1)
            hop(3, 1, 0, 0, -1)
            have(3, 0)
            spread_y((1, 1), (3, 1))
            have(1, 3)
            hop(1, 0, 0, -1, 0)
            hop(3, 0, 1, 1, 0)
        elif k == 3:
            have(1, 2)
            have(3, 3)
            hop(1, 3, 1, 0, 1)
            hop(3, 3, 1, 0, 1)
            have(3, 1)
        elif k == 4:
            have(2, 0)
            spread_y((2, 0), (2, 1))
            have(3, 2)
        elif k == 5:
            have(2, 1)
            hop(2, 1, 0, 0, -1)
            have(2, 3)
            hop(2, 3, 1, 0, 1)
            spread_y((0, 0), (0, 1))
        elif k == 6:
            have(0, 1)
            hop(0, 1, 0, 0, -1)
            have(0, 3)
            hop(0, 3, 1, 0, 1)
        elif k == 7:
            have(2, 2)
        elif k == 8:
            have(0, 2)

    def first_y(k):
        if k == 0:
            spread_x(0, 0)
            spread_y((0, 0))
            spread_y((0, 1))
            spread_x(0, 1)
        elif k == 1:
            have(1, 0)
            got(slot(0, 1), 0)
            spread_x(1, 0)
            hop(0, 1, 0, 0, -1)
            got(slot(0, 3), 0)
            spread_x(3, 0)
        elif k == 2:
            share(OWN)
            got(slot(0, 2), 0)
            spread_x(2, 0)
            for dy in (1, 3):
                got(slot(0, dy), 1)
                share(slot(0, dy))
                spread_x(dy, 1)
            hop(0, 3, 1, 0, 1)
            have(1, 1)
            have(1, 3)
        elif k == 3:
            got(slot(0, 2), 1)
            share(slot(0, 2))
            spread_x(2, 1)
            have(1, 2)
            have(3, 0)
            for dy in (0, 1, 3, 2):
                hop(1, dy, 0, -1, 0)
        elif k == 4:
            for dy in (1, 3, 2):
                have(3, dy)
            for dy in (0, 1, 3, 2):
                hop(3, dy, 1, 1, 0)
        elif k == 7:
            for dy in (2, 1, 3, 0):
                have(2, dy)

    def gather(k):
        pl.when(c == 0)(functools.partial(first_x, k))
        pl.when(c == 1)(functools.partial(first_y, k))

    gather(0)
    for dev in rows:
        rdma(sq.at[row], sq.at[row], sq_send, sq_recv.at[row], dev).start()
    rdma(wg_ref.at[:, :, columns(1 - c)], raw.at[c], w_send, w_recv, sibling).start()

    def deal(core):
        @pl.loop(0, KB // 64)
        def _(n):
            ks = pl.ds(pl.multiple_of(n * 64, 64), 64)
            both = jnp.swapaxes(raw[core, ks], 0, 1)
            w[core, ks, 0:FH] = both[0]
            w[core, ks, FH:2 * FH] = both[1]

    own_w.wait()
    deal(c)
    def digit(n):
        return (1 + 3 * (n % 2)) * (1 + 15 * (n // 2))

    def offsets(i):
        g, j = i // 4, i % 4
        far_first = g // 2
        order = 180 - 126 * far_first
        dx = 45 // digit(g) % 4
        dy = order // digit(j) % 4
        return dx, dy

    def rows_of(d):
        return pl.ds(pl.multiple_of(lax.rem(z + d + 4, 4) * ROWS, ROWS), ROWS)

    def scales():
        for d in range(1, 8):
            r = lax.rem(row + d, 8)
            wait_recv(sq.at[r], sq_recv.at[r])
        total = sq[0]
        for r in range(1, 8):
            total = total + sq[r]
        scale = jnp.broadcast_to(lax.rsqrt(total[0:1] / D + 1e-05), (128, 128)).T
        for q in range(4):
            sc[OWN, q] = scale[q * ROWS:(q + 1) * ROWS]

        def give(dx, dy, q, n):
            dst = lax.rem(dx + 4, 4) * 4 + dy
            dev = at_xy(x - dx, y - dy)
            rdma(sc.at[OWN, q], sc.at[dst, q], sc_send, sc_recv.at[dst, n], dev).start()

        for dy in range(4):
            for n in range(2):
                give(1 + 2 * (z // 2), dy, 2 * n + z % 2, n)
        for dx, dy in ((2, 0), (2, 1), (2, 2), (2, 3), (0, 1), (0, 2), (0, 3)):
            give(dx, dy, z, 0)

    gather(1)
    wait_recv(raw.at[1 - c], w_recv)
    deal(1 - c)

    gate, up = slice(0, FH), slice(FH, 2 * FH)
    mine = columns(c)

    def first_matmul(i):
        dx, dy = offsets(i)
        at = dx * 4 + dy
        wait_recv(a.at[at, 1 - c], as_recv.at[at])

        def tile(n):
            cols = pl.ds(pl.multiple_of(n * 256, 256), 256)
            p = jnp.dot(a[at, 0], w[0, :, cols], preferred_element_type=F32)
            p += jnp.dot(a[at, 1], w[1, :, cols], preferred_element_type=F32)
            s[i, :, cols] = p.astype(BF)

        pl.loop(0, 4)(tile)
        rdma(s.at[i, rows_of(2), gate], br.at[i, 0], b_send, b_recv.at[i, 0], at_z(1)).start()
        rdma(s.at[i, rows_of(-1), gate], br.at[i, 3], b_send, b_recv.at[i, 3], at_z(-1)).start()
        pl.loop(4, 7)(tile)
        rdma(s.at[i, rows_of(2), up], br.at[i, 1], b_send, b_recv.at[i, 1], at_z(-1)).start()
        rdma(s.at[i, rows_of(1), up], br.at[i, 2], b_send, b_recv.at[i, 2], at_z(1)).start()

    def combine(i):
        for n, d, cols in ((0, 1, gate), (1, -1, up)):
            wait_recv(br.at[i, n], b_recv.at[i, n])
            cs[i, n] = (s[i, rows_of(d), cols].astype(F32) + br[i, n].astype(F32)).astype(BF)
            rdma(cs.at[i, n], br.at[i, 4 + n], cs_send, b_recv.at[i, 4 + n], at_z(d)).start()

    def finish(i):
        for n in (2, 3, 4, 5):
            wait_recv(br.at[i, n], b_recv.at[i, n])
        dx, dy = offsets(i)
        mixed, n = 1 - i // 8, i // 4
        at = (mixed * (1 + 2 * (z // 2)) + (1 - mixed) * dx) * 4 + dy
        q = mixed * (2 * n + z % 2) + (1 - mixed) * z

        @pl.when(at != OWN)
        def _():
            wait_recv(sc.at[at, q], sc_recv.at[at, mixed * n])

        scale = sc[at, q]
        for k in range(FH // 128):
            cols = slice(k * 128, (k + 1) * 128)
            ups = slice(FH + k * 128, FH + (k + 1) * 128)
            g = (wide(s[i, rows_of(0), cols]) + wide(br[i, 4, :, cols]) + wide(br[i, 3, :, cols])) * scale
            u = (wide(s[i, rows_of(0), ups]) + wide(br[i, 5, :, cols]) + wide(br[i, 2, :, cols])) * scale
            to = pl.ds(pl.multiple_of(c * FH + k * 128, 128), 128)
            hid[i, rows_of(0), to] = (g / (1.0 + jnp.exp(-g)) * u).astype(BF)
        block = hid.at[i, rows_of(0), mine]
        rdma(block, block, c_send, c_recv.at[i, 0], at_z(1)).start()
        rdma(block, block, c_send, c_recv.at[i, 1], at_z(-1)).start()

    def half_rows(d, n):
        return pl.ds(pl.multiple_of(lax.rem(z + d + 4, 4) * ROWS + n * 16, 16), 16)

    def forward(i):
        for n, d in ((0, -1), (1, 1)):
            wait_recv(hid.at[i, rows_of(d), mine], c_recv.at[i, n])
            block = hid.at[i, half_rows(d, n), mine]
            rdma(block, block, c_send, c_recv.at[i, 2 + n], at_z(-d)).start()

    def pair(i):
        for n in (0, 1):
            wait_recv(hid.at[i, half_rows(2, n), mine], c_recv.at[i, 2 + n])
        block = hid.at[i, :, mine]
        rdma(block, block, hs_send, hs_recv.at[i], sibling).start()

    def second_matmul(i):
        wait_recv(hid.at[i, :, columns(1 - c)], hs_recv.at[i])

        @pl.loop(0, KB // 256)
        def _(n):
            cols = pl.ds(pl.multiple_of(n * 256, 256), 256)
            t = jnp.dot(hid[i], wd[:, cols], preferred_element_type=F32)
            ds[i, :, cols] = t.astype(BF)

    def ring(d):
        return at_xy(x, y + d)

    def line(d):
        return at_xy(x + d, y)

    top, low = slice(0, half), slice(half, TOK)

    def y_far(g, i):
        rdma(ds.at[i, top], df.at[g, 0], d_send, y_recv.at[g, 0], ring(1)).start()
        rdma(ds.at[i, low], df.at[g, 1], d_send, y_recv.at[g, 1], ring(-1)).start()

    def y_near(g, i, n):
        halves = (top, low)
        dev = ring(1 - 2 * n)
        rest = halves[1 - n]
        rdma(ds.at[i, rest], dn.at[g, n, rest], d_send, y_recv.at[g, 4 + n], dev).start()
        rows = halves[n]
        wait_recv(df.at[g, n], y_recv.at[g, n])
        ds[i, rows] = (wide(ds[i, rows]) + wide(df[g, n])).astype(BF)
        rdma(ds.at[i, rows], dn.at[g, n, rows], d_send, y_recv.at[g, 2 + n], dev).start()

    def y_got(g):
        for n in range(2):
            halves = (top, low)
            wait_recv(dn.at[g, n, halves[1 - n]], y_recv.at[g, 4 + n])
            wait_recv(dn.at[g, n, halves[n]], y_recv.at[g, 2 + n])

    def y_sum(g, i):
        y_got(g)
        ys[g] = (wide(ds[i]) + wide(dn[g, 0]) + wide(dn[g, 1])).astype(BF)

    def x_far():
        rdma(ys.at[2, top], xf.at[0], d_send, x_recv.at[0], line(1)).start()
        rdma(ys.at[2, low], xf.at[1], d_send, x_recv.at[1], line(-1)).start()

    def x_near(n):
        rows = (top, low)[n]
        wait_recv(xf.at[n], x_recv.at[n])
        ys[n, rows] = (wide(ys[n, rows]) + wide(xf[n])).astype(BF)
        for m in range(2):
            to = xn.at[n, (top, low)[m]]
            rdma(ys.at[m, rows], to, d_send, x_recv.at[2 + 2 * n + m], line(1 - 2 * n)).start()

    def branch_sums(t):
        def when(n, *bodies):
            @pl.when(t == LAG + n)
            def _():
                for body in bodies:
                    body()

        call = functools.partial
        for g in (0, 1):
            i = 4 * g
            when(i + 3, call(y_far, g, i + 3))
            when(i + 4, call(y_near, g, i + 1, 0), call(y_near, g, i + 2, 1))
            when(i + 6, call(y_sum, g, i))
        for g in (2, 3):
            i = 4 * g
            when(i, call(y_far, g, i))
            when(i + 1, call(y_near, g, i + 1, 0))
            when(i + 2, call(y_near, g, i + 2, 1))
        when(11, call(y_sum, 2, 11), x_far)
        when(13, call(x_near, 0), call(x_near, 1))

    def at(i, low, high, body):
        @pl.when(jnp.logical_and(i >= low, i < high))
        def _():
            body(i - low)

    def step(t, carry):
        pl.when(t == 1)(scales)
        at(t, COMBINE, STEPS + COMBINE, combine)
        at(t, FINISH, STEPS + FINISH, finish)
        at(t, FORWARD, STEPS + FORWARD, forward)
        at(t, PAIR, STEPS + PAIR, pair)
        for k in range(2, 9):
            pl.when(t == k - 1)(functools.partial(gather, k))
        at(t, 0, STEPS, first_matmul)
        pl.when(t == LAG)(own_wd.wait)
        at(t, LAG, STEPS + LAG, second_matmul)
        branch_sums(t)
        return carry

    lax.fori_loop(0, STEPS + LAG, step, 0)
    total = acc[...] + wide(ds[STEPS - 1])
    for n in range(2):
        for m in range(2):
            wait_recv(xn.at[n, (top, low)[m]], x_recv.at[2 + 2 * n + m])
        total += wide(xn[n])
    y_got(3)
    for n in range(2):
        total += wide(dn[3, n])
    out_ref[...] = total.astype(BF)

    wait_send(sq.at[0:7], sq_send)
    wait_send(raw.at[c], w_send)
    wait_send(sc.at[1:16, 0], sc_send)
    wait_send(a.at[0:15, c], a_send)
    wait_send(a.at[:, c], as_send)
    wait_send(s.at[:, :, gate], b_send)
    wait_send(cs, cs_send)
    wait_send(hid.at[:, 0:3 * ROWS, gate], c_send)
    wait_send(hid.at[:, :, gate], hs_send)
    wait_send(ds.at[0:15], d_send)


def local(hidden_state, norm_gain, gate_up_weight, down_weight):
    dma = pltpu.SemaphoreType.DMA
    any_, vmem = pl.BlockSpec(memory_space=pl.ANY), pl.BlockSpec(memory_space=pltpu.VMEM)
    return pl.pallas_call(
        kernel,
        out_shape=jax.ShapeDtypeStruct((TOK, KB), BF),
        in_specs=[vmem, vmem, any_, any_],
        out_specs=vmem,
        scratch_shapes=[
            pltpu.VMEM((STEPS, 2, TOK, KB), BF),
            pltpu.VMEM((2, KB, 2, FH), BF),
            pltpu.VMEM((2, KB, 2 * FH), BF),
            pltpu.VMEM((2 * FH, KB), BF),
            pltpu.VMEM((STEPS, TOK, 2 * FH), BF),
            pltpu.VMEM((STEPS, 6, ROWS, FH), BF),
            pltpu.VMEM((STEPS, 2, ROWS, FH), BF),
            pltpu.VMEM((STEPS, TOK, 2 * FH), BF),
            pltpu.VMEM((STEPS, TOK, KB), BF),
            pltpu.VMEM((4, 2, TOK // 2, KB), BF),
            pltpu.VMEM((4, 2, TOK, KB), BF),
            pltpu.VMEM((3, TOK, KB), BF),
            pltpu.VMEM((2, TOK // 2, KB), BF),
            pltpu.VMEM((2, TOK, KB), BF),
            pltpu.VMEM((TOK, KB), F32),
            pltpu.VMEM((8, 8, 128), F32),
            pltpu.VMEM((STEPS, 4, ROWS, 128), F32),
            dma, dma((8,)), dma, dma((STEPS, 2)), dma, dma((STEPS, 2)), dma, dma((STEPS,)),
            dma, dma, dma, dma,
            dma, dma((STEPS, 6)), dma, dma((STEPS, 4)), dma, dma, dma((STEPS,)), dma, dma((4, 6)), dma((6,)),
        ],
        compiler_params=pltpu.CompilerParams(
            collective_id=0, has_side_effects=True, vmem_limit_bytes=60 * 1024 * 1024
        ),
    )(hidden_state, norm_gain.reshape(1, KB), gate_up_weight, down_weight)


def solution(mesh):
    return jax.shard_map(
        local,
        mesh=mesh,
        in_specs=(
            P(("col", "depth"), "row"),
            P("row"),
            P("row", None, ("col", "depth")),
            P(("col", "depth"), "row"),
        ),
        out_specs=P(("col", "depth"), "row"),
        check_vma=False,
    )
```
